32 devices in a mesh: dp: 4 (over y, core), row: 8 (over z, x).
Axes of the slice: x: 2, y: 2, z: 4, core: 2. Of those that a mesh axis runs over, the one named last changes fastest.
Arguments:
- features: bfloat16 [4, 32, 256, 768], P('dp', 'row'), may hold values from -6 to 6
- cotangent: bfloat16 [4, 32, 256, 384], P('dp', 'row'), may hold values from -6 to 6
- projections: bfloat16 [3, 768, 384], P(None, 'dp'), may hold values from -0.21875 to 0.21875
- depths: int32 [4], replicated, may hold values from 1 to 32, as said below
Outputs:
- attended: bfloat16 [4, 32, 256, 384], P('dp', 'row')
- input_gradient: bfloat16 [4, 32, 256, 768], P('dp', 'row')
The draws below stay inside these ranges and needn't reach their ends.
Inputs may be any that keep to these rules, and one draw needn't show every extreme that they name: `depths`: one MSA has depth 32 and another depth 1.
All inputs are finite; a program needn't handle non-finite values.
Results may differ from the reference program's by a relative error of at most 0.006.
The reference program's roundings to bfloat16 on the way (of `probs_b` and `dlogits`) count: a program that leaves them out, or rounds other values in their place, can miss the bound.
Values may be sent and summed in bfloat16 or wider, within the bound.
A program may use at most 64 MiB of HBM per device.

```python
import jax
import jax.numpy as jnp
from jax import lax

MODEL_WIDTH = 768
HEADS = 6
HEAD_DIM = 64
ALIGNMENT_COLUMNS = 256
HEADS_WIDTH = 384
ALIGNMENT_COUNT = 4
MAXIMUM_DEPTH = 32


def draw_depths(key, part):
    key = jax.random.fold_in(key, 5)
    first_alignment, second_alignment = jax.random.split(key)
    base_offset = jax.random.randint(first_alignment, (ALIGNMENT_COUNT,), 1, MAXIMUM_DEPTH + 1, dtype=jnp.int32)
    deepest_alignment = jax.random.randint(second_alignment, (), 0, ALIGNMENT_COUNT, dtype=jnp.int32)
    shallow_alignment = (deepest_alignment + 1) % ALIGNMENT_COUNT
    column_positions = jnp.arange(ALIGNMENT_COUNT, dtype=jnp.int32)
    base_offset = jnp.where(column_positions == deepest_alignment, MAXIMUM_DEPTH, base_offset)
    return jnp.where(column_positions == shallow_alignment, 1, base_offset).astype(jnp.int32)


def draw_features(key, part):
    key = jax.random.fold_in(key, 11)
    rough_key = jax.random.fold_in(key, 0)
    array_shape = (ALIGNMENT_COUNT, MAXIMUM_DEPTH, ALIGNMENT_COLUMNS, MODEL_WIDTH)
    rough = jax.random.normal(rough_key, array_shape, jnp.float32)
    return jnp.clip(rough, -6.0, 6.0).astype(jnp.bfloat16)


def block_levels(key, extent, cuts, least, top_value):
    loudness = 1.0
    for axis_at, blocks in cuts:
        steps = jax.random.uniform(jax.random.fold_in(jax.random.fold_in(key, 6), axis_at), (blocks,), jnp.float32, least / len(cuts), top_value / len(cuts))
        loudness = loudness * jnp.repeat(jnp.exp(steps), extent[axis_at] // blocks).reshape((-1,) + (1,) * (len(extent) - 1 - axis_at))
    return loudness


def bell_draw(own_key, dims, scale, bound, cuts=(), kind=jnp.bfloat16):
    drawn = scale * jax.random.normal(own_key, dims, jnp.float32)
    if cuts:
        drawn = drawn * block_levels(own_key, dims, cuts, -0.22, 0.18)
    return jnp.clip(drawn, -bound, bound).astype(kind)


def setup_inputs(seed: int = 0) -> dict:
    splits = jax.random.split(jax.random.key(seed), 5)
    features = draw_features(jax.random.fold_in(splits[4], 71), 0)
    cotangent = bell_draw(splits[1], (ALIGNMENT_COUNT, MAXIMUM_DEPTH, ALIGNMENT_COLUMNS, HEADS_WIDTH), 1.0, 6.0, ((0, 4), (1, 8)))
    projections = bell_draw(splits[2], (3, MODEL_WIDTH, HEADS_WIDTH), MODEL_WIDTH ** -0.5, 0.21875, ((1, 4),))
    depths = draw_depths(jax.random.fold_in(splits[4], 71), 0)
    return dict(features=features, cotangent=cotangent, projections=projections, depths=depths)


def single_alignment(alignment_items, projections):
    rows_in, grads_in, depth = alignment_items
    slots_all = rows_in.shape[0]
    live = (jnp.arange(slots_all, dtype=jnp.int32) < depth).astype(jnp.float32)
    scale = 1.0 / jnp.sqrt(jnp.float32(HEAD_DIM) * depth.astype(jnp.float32))
    flat = rows_in.reshape(slots_all * ALIGNMENT_COLUMNS, MODEL_WIDTH)
    shaped = (slots_all, ALIGNMENT_COLUMNS, HEADS, HEAD_DIM)
    queries = jnp.dot(flat, projections[0], preferred_element_type=jnp.float32).astype(jnp.bfloat16).reshape(shaped)
    keys = jnp.dot(flat, projections[1], preferred_element_type=jnp.float32).astype(jnp.bfloat16).reshape(shaped)
    values = jnp.dot(flat, projections[2], preferred_element_type=jnp.float32).astype(jnp.bfloat16).reshape(shaped)
    mask = live[:, None, None, None]
    masked_queries = queries.astype(jnp.float32) * mask
    masked_grads = grads_in.reshape(shaped).astype(jnp.float32) * mask
    keys_f = keys.astype(jnp.float32)
    values_f = values.astype(jnp.float32)
    logits = jnp.einsum('rihd,rjhd->hij', masked_queries, keys_f) * scale
    top = lax.optimization_barrier(jnp.max(logits, axis=-1, keepdims=True))
    expo = jnp.exp(logits - top)
    probs = expo / lax.optimization_barrier(jnp.sum(expo, axis=-1, keepdims=True))
    probs_b = probs.astype(jnp.bfloat16).astype(jnp.float32)
    attended = (jnp.einsum('hij,rjhd->rihd', probs_b, values_f) * mask).astype(jnp.bfloat16)
    dprobs = jnp.einsum('rihd,rjhd->hij', masked_grads, values_f)
    inner = lax.optimization_barrier(jnp.sum(probs * dprobs, axis=-1, keepdims=True))
    dlogits = (probs * (dprobs - inner) * scale).astype(jnp.bfloat16).astype(jnp.float32)
    dvalues = jnp.einsum('hij,rihd->rjhd', probs_b, masked_grads).astype(jnp.bfloat16)
    dqueries = jnp.einsum('hij,rjhd->rihd', dlogits, keys_f).astype(jnp.bfloat16)
    dkeys = jnp.einsum('hij,rihd->rjhd', dlogits, masked_queries).astype(jnp.bfloat16)
    width = HEADS * HEAD_DIM
    total = jnp.dot(dqueries.reshape(-1, width), projections[0].T, preferred_element_type=jnp.float32)
    total = total + jnp.dot(dkeys.reshape(-1, width), projections[1].T, preferred_element_type=jnp.float32)
    total = total + jnp.dot(dvalues.reshape(-1, width), projections[2].T, preferred_element_type=jnp.float32)
    input_gradient = (total.reshape(slots_all, ALIGNMENT_COLUMNS, MODEL_WIDTH) * live[:, None, None]).astype(jnp.bfloat16)
    return (attended.reshape(slots_all, ALIGNMENT_COLUMNS, width), input_gradient)

def reference(features, cotangent, projections, depths):
    attended, input_gradient = lax.map(lambda alignment_items: single_alignment(alignment_items, projections), (features, cotangent, depths.astype(jnp.int32)))
    return (attended, input_gradient)
```

```python
import functools

import jax
import jax.numpy as jnp
from jax import lax
from jax.experimental import pallas as pl
from jax.experimental.pallas import tpu as pltpu
from jax.sharding import PartitionSpec as P

HEADS = 6
F32 = jnp.float32
BF16 = jnp.bfloat16
MESH = pl.DeviceIdType.MESH
LAST = (((1,), (1,)), ((), ()))
FIRST = (((0,), (0,)), ((), ()))


def nt(a, b):
    return lax.dot_general(a, b, LAST, preferred_element_type=F32)


def tn(a, b):
    return lax.dot_general(a, b, FIRST, preferred_element_type=F32)


def nn(a, b):
    return jnp.dot(a, b, preferred_element_type=F32)


def gather_copies(dp):
    bits = []
    b = dp // 2
    while b:
        bits.append(b)
        b //= 2
    pairs = []
    for k, b in enumerate(bits):
        masks = [0]
        for hi in bits[:k]:
            masks += [m | hi for m in masks]
        pairs += [(m, b) for m in masks]
    return bits, pairs


def flip(me, mask):
    b = 1
    out = me
    while b <= mask:
        if mask & b:
            out = out + b - 2 * b * (lax.div(me, b) % 2)
        b *= 2
    return out


def live_of(depth, slot):
    return (slot < depth).astype(F32)


def tied_kernel(
    dp, ring, sub, gsub,
    feats_hbm, cot_hbm, proj_hbm, depths,
    qc_out, kc_out, vc_out, gc_out, wg_out, pd_out,
    feats, cot, wg, qc, kc, vc, gc, part, recv, pd,
    load_sem, store_sem, w_send, w_recv, r_send, r_recv, g_send, g_recv,
):
    me = lax.axis_index("dp")
    row = lax.axis_index("row")
    slots, cols, _ = feats.shape
    inner = cot.shape[2]
    hd = inner // HEADS
    shard = proj_hbm.shape[1]
    rows = part.shape[0] // ring
    half = rows // 2
    piece = half // sub
    lines = ring // 2

    def row_at(pos):
        z0 = pos
        z1 = ring - 1 - pos
        low = (pos < lines).astype(jnp.int32)
        return low * (2 * z0) + (1 - low) * (2 * z1 + 1)

    z = row // 2
    x = row % 2
    pos = z + x * (ring - 1 - 2 * z)
    right = row_at((pos + 1) % ring)
    left = row_at((pos + ring - 1) % ring)

    def shard_at(idx):
        return wg.at[:, pl.ds(pl.multiple_of(idx * shard, shard), shard), :]

    loads = [
        pltpu.make_async_copy(proj_hbm, shard_at(me), load_sem.at[0]),
        pltpu.make_async_copy(feats_hbm.at[0], feats, load_sem.at[1]),
        pltpu.make_async_copy(cot_hbm.at[0], cot, load_sem.at[2]),
    ]
    for c in loads:
        c.start()

    bits, pairs = gather_copies(dp)
    barrier = pltpu.get_barrier_semaphore()
    for b in bits:
        pl.semaphore_signal(barrier, inc=1, device_id=(flip(me, b), row), device_id_type=MESH)
    for n in (left, right):
        pl.semaphore_signal(barrier, inc=1, device_id=(me, n), device_id_type=MESH)
    pl.semaphore_wait(barrier, len(bits) + 2)

    def weight_copy(m, b):
        i = pairs.index((m, b))
        src = shard_at(flip(me, m))
        return pltpu.make_async_remote_copy(
            src_ref=src, dst_ref=src, send_sem=w_send.at[i], recv_sem=w_recv.at[i],
            device_id=(flip(me, b), row), device_id_type=MESH,
        )

    loads[0].wait()
    for b in bits:
        weight_copy(0, b).start()
    for m, b in pairs:
        weight_copy(m, b).wait_recv()
        for lower in bits:
            if lower < b:
                weight_copy(m | b, lower).start()
    loads[1].wait()
    loads[2].wait()

    depth = depths[me]
    first = row * slots
    for r in range(0, slots, 2):
        live = [live_of(depth, first + r + k) for k in range(2)]
        for p, dest in enumerate((qc, kc, vc, gc)):
            if p < 3:
                vals = [nn(feats[r + k], wg[p]) for k in range(2)]
            else:
                vals = [cot[r + k].astype(F32) for k in range(2)]
            if p == 0 or p == 3:
                vals = [v * l for v, l in zip(vals, live)]
            vals = [v.astype(BF16) for v in vals]
            for h in range(HEADS):
                dest[h, :, r * hd:(r + 2) * hd] = jnp.concatenate(
                    [v[:, h * hd:(h + 1) * hd] for v in vals], axis=1
                )

    stores = [
        pltpu.make_async_copy(s, d, store_sem.at[i])
        for i, (s, d) in enumerate(
            ((qc, qc_out), (kc, kc_out), (vc, vc_out), (gc, gc_out), (wg, wg_out))
        )
    ]

    for h in range(HEADS):
        at = slice(h * cols, (h + 1) * cols)
        part[at, 0:cols] = nt(qc[h], kc[h])
        part[at, cols:2 * cols] = nt(gc[h], vc[h])

    def part_rows(chunk, d, u):
        start = pl.multiple_of(chunk * rows + (d * half + u * piece), 8)
        return pl.ds(start, piece)

    def ring_copy(s, d, u):
        chunk = (pos + ring - 1 - s) % ring if d == 0 else (pos + 1 + s) % ring
        if s == 0:
            src = part.at[part_rows(chunk, d, u)]
        else:
            src = recv.at[d, s - 1, u]
        return pltpu.make_async_remote_copy(
            src_ref=src, dst_ref=recv.at[d, s, u],
            send_sem=r_send.at[d, s, u], recv_sem=r_recv.at[d, s, u],
            device_id=(me, right if d == 0 else left), device_id_type=MESH,
        )

    for u in range(sub):
        for d in range(2):
            ring_copy(0, d, u).start()
    for c in stores:
        c.start()
    for s in range(ring - 2):
        for u in range(sub):
            for d in range(2):
                ring_copy(s, d, u).wait_recv()
                chunk = (pos + 2 * ring - 2 - s) % ring if d == 0 else (pos + 2 + s) % ring
                recv[d, s, u] = recv[d, s, u] + part[part_rows(chunk, d, u)]
                ring_copy(s + 1, d, u).start()

    norm = lax.broadcast_in_dim(depth.astype(F32) * float(hd), (8, 128), ())
    scale = (1.0 / jnp.sqrt(norm))[0:1, 0:1]
    lastst = ring - 2

    def finish(d, u):
        ring_copy(lastst, d, u).wait_recv()
        total = recv[d, lastst, u] + part[part_rows(pos, d, u)]
        logits = total[:, 0:cols] * scale
        dprobs = total[:, cols:2 * cols]
        top = jnp.max(logits, axis=-1, keepdims=True)
        expo = jnp.exp(logits - top)
        probs = expo / jnp.sum(expo, axis=-1, keepdims=True)
        mean = jnp.sum(probs * dprobs, axis=-1, keepdims=True)
        return probs.astype(BF16), (probs * (dprobs - mean) * scale).astype(BF16)

    grow = rows // gsub

    def pd_rows(chunk, g):
        return pl.ds(pl.multiple_of(chunk * rows + g * grow, 16), grow)

    def spread_copy(s, d, g):
        chunk = (pos + ring - s) % ring if d == 0 else (pos + s) % ring
        ref = pd.at[pd_rows(chunk, g)]
        return pltpu.make_async_remote_copy(
            src_ref=ref, dst_ref=ref,
            send_sem=g_send.at[d, s, g], recv_sem=g_recv.at[d, s, g],
            device_id=(me, right if d == 0 else left), device_id_type=MESH,
        )

    def hops(d):
        out = []
        for s in range(lines):
            for g in range(gsub):
                if s < lines - 1 or (d == 0 and g == 0) or (d == 1 and g == 1):
                    out.append((s, g))
        return out

    def put(d):
        done = [finish(d, u) for u in range(sub)]
        probs = jnp.concatenate([a for a, _ in done], axis=0)
        dlog = jnp.concatenate([b for _, b in done], axis=0)
        return probs, dlog

    if gsub == 2:
        for d in range(2):
            probs, dlog = put(d)
            pd[pd_rows(pos, d), 0:cols] = probs
            pd[pd_rows(pos, d), cols:2 * cols] = dlog
            for e in range(2):
                if (0, d) in hops(e):
                    spread_copy(0, e, d).start()
    else:
        a, b = put(0), put(1)
        pd[pd_rows(pos, 0), 0:cols] = jnp.concatenate([a[0], b[0]], axis=0)
        pd[pd_rows(pos, 0), cols:2 * cols] = jnp.concatenate([a[1], b[1]], axis=0)
        for e in range(2):
            if (0, 0) in hops(e):
                spread_copy(0, e, 0).start()

    for s in range(lines):
        for g in range(gsub):
            for e in range(2):
                if (s, g) in hops(e):
                    spread_copy(s, e, g).wait_recv()
                    if (s + 1, g) in hops(e):
                        spread_copy(s + 1, e, g).start()

    last_store = pltpu.make_async_copy(pd, pd_out, store_sem.at[5])
    last_store.start()
    for m, b in pairs:
        weight_copy(m, b).wait_send()
    for s in range(ring - 1):
        for u in range(sub):
            for d in range(2):
                ring_copy(s, d, u).wait_send()
    for e in range(2):
        for s, g in hops(e):
            spread_copy(s, e, g).wait_send()
    for c in stores:
        c.wait()
    last_store.wait()


def output_kernel(qc, kc, vc, gc, wg, pd, depths, att, grad, stacked):
    slots, cols, inner = att.shape[1:]
    hd = inner // HEADS
    depth = depths[lax.axis_index("dp")]
    first = lax.axis_index("row") * slots
    live = [live_of(depth, first + r) for r in range(slots)]
    for h in range(0, HEADS, 2):
        got = []
        for k in range(2):
            n = h + k
            at = slice(n * cols, (n + 1) * cols)
            probs = pd[at, 0:cols]
            dlog = pd[at, cols:2 * cols]
            got.append((
                nn(probs, vc[n]),
                nn(dlog, kc[n]).astype(BF16),
                tn(dlog, qc[n]).astype(BF16),
                tn(probs, gc[n]).astype(BF16),
            ))
        lanes = slice(h * hd, (h + 2) * hd)
        for r in range(slots):
            cut = slice(r * hd, (r + 1) * hd)
            both = [jnp.concatenate([g[i][:, cut] for g in got], axis=1) for i in range(4)]
            att[0, r, :, lanes] = (both[0] * live[r]).astype(BF16)
            for i in range(3):
                stacked[i, r, :, lanes] = both[i + 1]
    for r in range(slots):
        total = nt(stacked[0, r], wg[0]) + nt(stacked[1, r], wg[1]) + nt(stacked[2, r], wg[2])
        grad[0, r] = (total * live[r]).astype(BF16)


def local(dp, ring, features, cotangent, projections, depths):
    _, slots, cols, width = features.shape
    inner = projections.shape[2]
    wide = slots * (inner // HEADS)
    rows = HEADS * cols // ring
    half = rows // 2
    sub = 2 if half % 16 == 0 else 1
    gsub = 2 if rows % 32 == 0 else 1
    _, pairs = gather_copies(dp)
    vmem = pl.BlockSpec(memory_space=pltpu.VMEM)
    anyspace = pl.BlockSpec(memory_space=pl.ANY)
    smem = pl.BlockSpec(memory_space=pltpu.SMEM)
    byhead = jax.ShapeDtypeStruct((HEADS, cols, wide), BF16)
    weights = (3, width, inner)
    pairshape = (HEADS * cols, 2 * cols)
    lines = ring // 2
    dma = pltpu.SemaphoreType.DMA
    *shaped, wg, pd = pl.pallas_call(
        functools.partial(tied_kernel, dp, ring, sub, gsub),
        out_shape=(
            byhead, byhead, byhead, byhead,
            jax.ShapeDtypeStruct(weights, BF16),
            jax.ShapeDtypeStruct(pairshape, BF16),
        ),
        in_specs=[anyspace, anyspace, anyspace, smem],
        out_specs=[anyspace] * 6,
        scratch_shapes=[
            pltpu.VMEM((slots, cols, width), BF16),
            pltpu.VMEM((slots, cols, inner), BF16),
            pltpu.VMEM(weights, BF16),
            *[pltpu.VMEM((HEADS, cols, wide), BF16)] * 4,
            pltpu.VMEM(pairshape, F32),
            pltpu.VMEM((2, ring - 1, sub, half // sub, 2 * cols), F32),
            pltpu.VMEM(pairshape, BF16),
            dma((3,)),
            dma((6,)),
            dma((len(pairs),)),
            dma((len(pairs),)),
            dma((2, ring - 1, sub)),
            dma((2, ring - 1, sub)),
            dma((2, lines, gsub)),
            dma((2, lines, gsub)),
        ],
        compiler_params=pltpu.CompilerParams(
            collective_id=0, has_side_effects=True, vmem_limit_bytes=40 * 2**20
        ),
    )(features, cotangent, projections, depths)
    return pl.pallas_call(
        output_kernel,
        out_shape=(
            jax.ShapeDtypeStruct((1, slots, cols, inner), BF16),
            jax.ShapeDtypeStruct((1, slots, cols, width), BF16),
        ),
        in_specs=[vmem] * 6 + [smem],
        out_specs=[vmem] * 2,
        scratch_shapes=[pltpu.VMEM((3, slots, cols, inner), BF16)],
        compiler_params=pltpu.CompilerParams(vmem_limit_bytes=40 * 2**20),
    )(*shaped, wg, pd, depths)


def solution(mesh):
    return jax.shard_map(
        functools.partial(local, mesh.shape["dp"], mesh.shape["row"]),
        mesh=mesh,
        in_specs=(P("dp", "row", None, None), P("dp", "row", None, None), P(None, "dp", None), P()),
        out_specs=(P("dp", "row", None, None), P("dp", "row", None, None)),
        check_vma=False,
    )
```

```python
import functools

import jax
import jax.numpy as jnp
from jax import lax
from jax.experimental import pallas as pl
from jax.experimental.pallas import tpu as pltpu
from jax.sharding import PartitionSpec as P

HEADS = 6
F32 = jnp.float32
BF16 = jnp.bfloat16
MESH = pl.DeviceIdType.MESH
LAST = (((1,), (1,)), ((), ()))
FIRST = (((0,), (0,)), ((), ()))


def nt(a, b):
    return lax.dot_general(a, b, LAST, preferred_element_type=F32)


def tn(a, b):
    return lax.dot_general(a, b, FIRST, preferred_element_type=F32)


def nn(a, b):
    return jnp.dot(a, b, preferred_element_type=F32)


def gather_copies(dp):
    bits = []
    b = dp // 2
    while b:
        bits.append(b)
        b //= 2
    pairs = []
    for k, b in enumerate(bits):
        masks = [0]
        for hi in bits[:k]:
            masks += [m | hi for m in masks]
        pairs += [(m, b) for m in masks]
    return bits, pairs


def flip(me, mask):
    b = 1
    out = me
    while b <= mask:
        if mask & b:
            out = out + b - 2 * b * (lax.div(me, b) % 2)
        b *= 2
    return out


def live_of(depth, slot):
    return (slot < depth).astype(F32)


def tied_kernel(
    dp, ring, gsub,
    feats_hbm, cot_hbm, proj_hbm, depths,
    qc_out, kc_out, vc_out, gc_out, wg_out, pd_out,
    feats, cot, wg, qc, kc, vc, gc, part, recv, pd,
    load_sem, store_sem, w_send, w_recv, r_send, r_recv, g_send, g_recv, g_store,
):
    me = lax.axis_index("dp")
    row = lax.axis_index("row")
    slots, cols, _ = feats.shape
    inner = cot.shape[2]
    hd = inner // HEADS
    shard = proj_hbm.shape[1]
    rows = part.shape[1] // ring
    half = rows // 2
    lines = ring // 2

    def row_at(pos):
        z0 = pos
        z1 = ring - 1 - pos
        low = (pos < lines).astype(jnp.int32)
        return low * (2 * z0) + (1 - low) * (2 * z1 + 1)

    z = row // 2
    x = row % 2
    pos = z + x * (ring - 1 - 2 * z)
    right = row_at((pos + 1) % ring)
    left = row_at((pos + ring - 1) % ring)

    groups = (slice(2 * inner, 3 * inner), slice(0, 2 * inner))

    def shard_at(idx, lanes):
        return wg.at[pl.ds(pl.multiple_of(idx * shard, shard), shard), lanes]

    loads = [
        pltpu.make_async_copy(
            proj_hbm.at[p], shard_at(me, slice(p * inner, (p + 1) * inner)), load_sem.at[p]
        )
        for p in range(3)
    ]
    loads.append(pltpu.make_async_copy(feats_hbm.at[0], feats, load_sem.at[3]))
    loads.append(pltpu.make_async_copy(cot_hbm.at[0], cot, load_sem.at[4]))
    for c in (loads[2], loads[0], loads[1], loads[3], loads[4]):
        c.start()

    bits, pairs = gather_copies(dp)
    barrier = pltpu.get_barrier_semaphore()
    for b in bits:
        pl.semaphore_signal(barrier, inc=1, device_id=(flip(me, b), row), device_id_type=MESH)
    for n in (left, right):
        pl.semaphore_signal(barrier, inc=1, device_id=(me, n), device_id_type=MESH)
    pl.semaphore_wait(barrier, len(bits) + 2)

    def weight_copy(t, m, b):
        i = pairs.index((m, b))
        src = shard_at(flip(me, m), groups[t])
        return pltpu.make_async_remote_copy(
            src_ref=src, dst_ref=src, send_sem=w_send.at[t, i], recv_sem=w_recv.at[t, i],
            device_id=(flip(me, b), row), device_id_type=MESH,
        )

    def weights_from(t, b):
        for m, at in pairs:
            if at == b:
                weight_copy(t, m, b).wait_recv()
                for lower in bits:
                    if lower < b:
                        weight_copy(t, m | b, lower).start()

    loads[2].wait()
    for b in bits:
        weight_copy(0, 0, b).start()
    weights_from(0, bits[0])
    loads[0].wait()
    loads[1].wait()
    for b in bits:
        weight_copy(1, 0, b).start()
    for b in bits[1:]:
        weights_from(0, b)

    depth = depths[me]
    first = row * slots

    def by_head(dest, vals, r):
        vals = [v.astype(BF16) for v in vals]
        for h in range(HEADS):
            dest[h, :, r * hd:(r + 2) * hd] = jnp.concatenate(
                [v[:, h * hd:(h + 1) * hd] for v in vals], axis=1
            )

    def live_at(r):
        return [live_of(depth, first + r + k) for k in range(2)]

    loads[3].wait()
    loads[4].wait()
    for r in range(0, slots, 2):
        by_head(gc, [cot[r + k].astype(F32) * l for k, l in enumerate(live_at(r))], r)
        by_head(vc, [nn(feats[r + k], wg[:, groups[0]]) for k in range(2)], r)
    for h in range(HEADS):
        part[0, h * cols:(h + 1) * cols, :] = nt(gc[h], vc[h])

    def part_rows(chunk, d):
        return pl.ds(pl.multiple_of(chunk * rows + d * half, 8), half)

    def ring_copy(s, d, u):
        chunk = (pos + ring - 1 - s) % ring if d == 0 else (pos + 1 + s) % ring
        if s == 0:
            src = part.at[u, part_rows(chunk, d)]
        else:
            src = recv.at[d, s - 1, u]
        return pltpu.make_async_remote_copy(
            src_ref=src, dst_ref=recv.at[d, s, u],
            send_sem=r_send.at[d, s, u], recv_sem=r_recv.at[d, s, u],
            device_id=(me, right if d == 0 else left), device_id_type=MESH,
        )

    def hop(s, u):
        for d in range(2):
            ring_copy(s, d, u).wait_recv()
            chunk = (pos + 2 * ring - 2 - s) % ring if d == 0 else (pos + 2 + s) % ring
            recv[d, s, u] = recv[d, s, u] + part[u, part_rows(chunk, d)]
            ring_copy(s + 1, d, u).start()

    for d in range(2):
        ring_copy(0, d, 0).start()
    weights_from(1, bits[0])
    hop(0, 0)
    for b in bits[1:]:
        weights_from(1, b)
    for r in range(0, slots, 2):
        both = [nn(feats[r + k], wg[:, groups[1]]) for k in range(2)]
        by_head(qc, [v[:, :inner] * l for v, l in zip(both, live_at(r))], r)
        by_head(kc, [v[:, inner:] for v in both], r)
        if r == 0:
            hop(1, 0)
    for h in range(HEADS):
        part[1, h * cols:(h + 1) * cols, :] = nt(qc[h], kc[h])
    for d in range(2):
        ring_copy(0, d, 1).start()

    stores = [
        pltpu.make_async_copy(s, d, store_sem.at[i])
        for i, (s, d) in enumerate(
            ((qc, qc_out), (kc, kc_out), (vc, vc_out), (gc, gc_out), (wg, wg_out))
        )
    ]
    for c in stores:
        c.start()
    for s in range(ring - 2):
        if s + 2 < ring - 2:
            hop(s + 2, 0)
        hop(s, 1)

    norm = lax.broadcast_in_dim(depth.astype(F32) * float(hd), (8, 128), ())
    scale = (1.0 / jnp.sqrt(norm))[0:1, 0:1]
    last = ring - 2

    def finish(d):
        for u in range(2):
            ring_copy(last, d, u).wait_recv()
        at = part_rows(pos, d)
        dprobs = recv[d, last, 0] + part[0, at]
        logits = (recv[d, last, 1] + part[1, at]) * scale
        top = jnp.max(logits, axis=-1, keepdims=True)
        expo = jnp.exp(logits - top)
        probs = expo / jnp.sum(expo, axis=-1, keepdims=True)
        mean = jnp.sum(probs * dprobs, axis=-1, keepdims=True)
        return probs.astype(BF16), (probs * (dprobs - mean) * scale).astype(BF16)

    grow = rows // gsub

    def pd_rows(chunk, g):
        return pl.ds(pl.multiple_of(chunk * rows + g * grow, 16), grow)

    def chunk_from(s, d):
        return (pos + ring - s) % ring if d == 0 else (pos + s) % ring

    def spread_copy(s, d, g):
        ref = pd.at[pd_rows(chunk_from(s, d), g)]
        return pltpu.make_async_remote_copy(
            src_ref=ref, dst_ref=ref,
            send_sem=g_send.at[d, s, g], recv_sem=g_recv.at[d, s, g],
            device_id=(me, right if d == 0 else left), device_id_type=MESH,
        )

    def keep_copy(s, d, g):
        at = pd_rows(chunk_from(s, d), g)
        return pltpu.make_async_copy(pd.at[at], pd_out.at[at], g_store.at[d, s, g])

    def sends(s, d, g):
        if s < lines - 1:
            return True
        return s == lines - 1 and d == g

    if gsub == 2:
        for d in range(2):
            probs, dlog = finish(d)
            pd[pd_rows(pos, d), 0:cols] = probs
            pd[pd_rows(pos, d), cols:2 * cols] = dlog
            for e in range(2):
                if sends(0, e, d):
                    spread_copy(0, e, d).start()
            keep_copy(0, 0, d).start()
    else:
        a, b = finish(0), finish(1)
        pd[pd_rows(pos, 0), 0:cols] = jnp.concatenate([a[0], b[0]], axis=0)
        pd[pd_rows(pos, 0), cols:2 * cols] = jnp.concatenate([a[1], b[1]], axis=0)
        for e in range(2):
            if sends(0, e, 0):
                spread_copy(0, e, 0).start()
        keep_copy(0, 0, 0).start()

    kept = [(0, 0, g) for g in range(gsub)]
    for s in range(lines):
        for g in range(gsub):
            for e in range(2):
                if sends(s, e, g):
                    spread_copy(s, e, g).wait_recv()
                    if sends(s + 1, e, g):
                        spread_copy(s + 1, e, g).start()
                    keep_copy(s + 1, e, g).start()
                    kept.append((s + 1, e, g))

    for t in range(2):
        for m, b in pairs:
            weight_copy(t, m, b).wait_send()
    for s in range(ring - 1):
        for u in range(2):
            for d in range(2):
                ring_copy(s, d, u).wait_send()
    for s in range(lines):
        for g in range(gsub):
            for e in range(2):
                if sends(s, e, g):
                    spread_copy(s, e, g).wait_send()
    for c in stores:
        c.wait()
    for s, e, g in kept:
        keep_copy(s, e, g).wait()


def output_kernel(qc, kc, vc, gc, wg, pd, depths, att, grad, stacked):
    slots, cols, inner = att.shape[1:]
    hd = inner // HEADS
    depth = depths[lax.axis_index("dp")]
    first = lax.axis_index("row") * slots
    live = [live_of(depth, first + r) for r in range(slots)]
    for h in range(0, HEADS, 2):
        got = []
        for k in range(2):
            n = h + k
            at = slice(n * cols, (n + 1) * cols)
            probs = pd[at, 0:cols]
            dlog = pd[at, cols:2 * cols]
            got.append((
                nn(probs, vc[n]),
                nn(dlog, kc[n]).astype(BF16),
                tn(dlog, qc[n]).astype(BF16),
                tn(probs, gc[n]).astype(BF16),
            ))
        lanes = slice(h * hd, (h + 2) * hd)
        for r in range(slots):
            cut = slice(r * hd, (r + 1) * hd)
            both = [jnp.concatenate([g[i][:, cut] for g in got], axis=1) for i in range(4)]
            att[0, r, :, lanes] = (both[0] * live[r]).astype(BF16)
            for i in range(3):
                stacked[r, :, i * inner + h * hd:i * inner + (h + 2) * hd] = both[i + 1]
    for r in range(slots):
        total = nt(stacked[r], wg[...])
        grad[0, r] = (total * live[r]).astype(BF16)


def local(dp, ring, features, cotangent, projections, depths):
    _, slots, cols, width = features.shape
    inner = projections.shape[2]
    wide = slots * (inner // HEADS)
    rows = HEADS * cols // ring
    gsub = 2 if rows % 32 == 0 else 1
    _, pairs = gather_copies(dp)
    vmem = pl.BlockSpec(memory_space=pltpu.VMEM)
    hbm = pl.BlockSpec(memory_space=pltpu.HBM)
    anyspace = pl.BlockSpec(memory_space=pl.ANY)
    smem = pl.BlockSpec(memory_space=pltpu.SMEM)
    byhead = jax.ShapeDtypeStruct((HEADS, cols, wide), BF16)
    weights = (width, 3 * inner)
    pairshape = (HEADS * cols, 2 * cols)
    lines = ring // 2
    dma = pltpu.SemaphoreType.DMA
    *shaped, wg, pd = pl.pallas_call(
        functools.partial(tied_kernel, dp, ring, gsub),
        out_shape=(
            byhead, byhead, byhead, byhead,
            jax.ShapeDtypeStruct(weights, BF16),
            jax.ShapeDtypeStruct(pairshape, BF16),
        ),
        in_specs=[hbm, hbm, hbm, smem],
        out_specs=[anyspace] * 6,
        scratch_shapes=[
            pltpu.VMEM((slots, cols, width), BF16),
            pltpu.VMEM((slots, cols, inner), BF16),
            pltpu.VMEM(weights, BF16),
            *[pltpu.VMEM((HEADS, cols, wide), BF16)] * 4,
            pltpu.VMEM((2, HEADS * cols, cols), F32),
            pltpu.VMEM((2, ring - 1, 2, rows // 2, cols), F32),
            pltpu.VMEM(pairshape, BF16),
            dma((5,)),
            dma((5,)),
            dma((2, len(pairs))),
            dma((2, len(pairs))),
            dma((2, ring - 1, 2)),
            dma((2, ring - 1, 2)),
            dma((2, lines, gsub)),
            dma((2, lines, gsub)),
            dma((2, lines + 1, gsub)),
        ],
        compiler_params=pltpu.CompilerParams(
            collective_id=0, has_side_effects=True, vmem_limit_bytes=40 * 2**20
        ),
    )(features, cotangent, projections, depths)
    return pl.pallas_call(
        output_kernel,
        out_shape=(
            jax.ShapeDtypeStruct((1, slots, cols, inner), BF16),
            jax.ShapeDtypeStruct((1, slots, cols, width), BF16),
        ),
        in_specs=[vmem] * 6 + [smem],
        out_specs=[vmem] * 2,
        scratch_shapes=[pltpu.VMEM((slots, cols, 3 * inner), BF16)],
        compiler_params=pltpu.CompilerParams(vmem_limit_bytes=40 * 2**20),
    )(*shaped, wg, pd, depths)


def solution(mesh):
    return jax.shard_map(
        functools.partial(local, mesh.shape["dp"], mesh.shape["row"]),
        mesh=mesh,
        in_specs=(P("dp", "row", None, None), P("dp", "row", None, None), P(None, "dp", None), P()),
        out_specs=(P("dp", "row", None, None), P("dp", "row", None, None)),
        check_vma=False,
    )
```

```python
import functools

import jax
import jax.numpy as jnp
from jax import lax
from jax.experimental import pallas as pl
from jax.experimental.pallas import tpu as pltpu
from jax.sharding import PartitionSpec as P

HEADS = 6
F32 = jnp.float32
BF16 = jnp.bfloat16
MESH = pl.DeviceIdType.MESH
LAST = (((1,), (1,)), ((), ()))
FIRST = (((0,), (0,)), ((), ()))


def nt(a, b):
    return lax.dot_general(a, b, LAST, preferred_element_type=F32)


def tn(a, b):
    return lax.dot_general(a, b, FIRST, preferred_element_type=F32)


def nn(a, b):
    return jnp.dot(a, b, preferred_element_type=F32)


def gather_copies(dp):
    bits = []
    b = dp // 2
    while b:
        bits.append(b)
        b //= 2
    pairs = []
    for k, b in enumerate(bits):
        masks = [0]
        for hi in bits[:k]:
            masks += [m | hi for m in masks]
        pairs += [(m, b) for m in masks]
    return bits, pairs


def flip(me, mask):
    b = 1
    out = me
    while b <= mask:
        if mask & b:
            out = out + b - 2 * b * (lax.div(me, b) % 2)
        b *= 2
    return out


def live_of(depth, slot):
    return (slot < depth).astype(F32)


def tied_kernel(
    dp, ring, gsub,
    feats_hbm, cot_hbm, proj_hbm, depths,
    att_out, stacked_out, wg_out,
    feats, cot, wg, qc, kc, vc, gc, part, recv, pd, made, att, stacked,
    load_sem, store_sem, w_send, w_recv, r_send, r_recv, g_send, g_recv,
):
    me = lax.axis_index("dp")
    row = lax.axis_index("row")
    slots, cols, _ = feats.shape
    inner = cot.shape[2]
    hd = inner // HEADS
    shard = proj_hbm.shape[1]
    rows = part.shape[1] // ring
    half = rows // 2
    lines = ring // 2

    def row_at(pos):
        z0 = pos
        z1 = ring - 1 - pos
        low = (pos < lines).astype(jnp.int32)
        return low * (2 * z0) + (1 - low) * (2 * z1 + 1)

    z = row // 2
    x = row % 2
    pos = z + x * (ring - 1 - 2 * z)
    right = row_at((pos + 1) % ring)
    left = row_at((pos + ring - 1) % ring)

    groups = (slice(2 * inner, 3 * inner), slice(0, 2 * inner))

    def shard_at(idx, lanes):
        return wg.at[pl.ds(pl.multiple_of(idx * shard, shard), shard), lanes]

    loads = [
        pltpu.make_async_copy(
            proj_hbm.at[p], shard_at(me, slice(p * inner, (p + 1) * inner)), load_sem.at[p]
        )
        for p in range(3)
    ]
    loads.append(pltpu.make_async_copy(feats_hbm.at[0], feats, load_sem.at[3]))
    loads.append(pltpu.make_async_copy(cot_hbm.at[0], cot, load_sem.at[4]))
    for c in (loads[2], loads[0], loads[1], loads[3], loads[4]):
        c.start()

    bits, pairs = gather_copies(dp)
    barrier = pltpu.get_barrier_semaphore()
    for b in bits:
        pl.semaphore_signal(barrier, inc=1, device_id=(flip(me, b), row), device_id_type=MESH)
    for n in (left, right):
        pl.semaphore_signal(barrier, inc=1, device_id=(me, n), device_id_type=MESH)
    pl.semaphore_wait(barrier, len(bits) + 2)

    def weight_copy(t, m, b):
        i = pairs.index((m, b))
        src = shard_at(flip(me, m), groups[t])
        return pltpu.make_async_remote_copy(
            src_ref=src, dst_ref=src, send_sem=w_send.at[t, i], recv_sem=w_recv.at[t, i],
            device_id=(flip(me, b), row), device_id_type=MESH,
        )

    def weights_from(t, b):
        for m, at in pairs:
            if at == b:
                weight_copy(t, m, b).wait_recv()
                for lower in bits:
                    if lower < b:
                        weight_copy(t, m | b, lower).start()

    loads[2].wait()
    for b in bits:
        weight_copy(0, 0, b).start()
    weights_from(0, bits[0])
    loads[0].wait()
    loads[1].wait()
    for b in bits:
        weight_copy(1, 0, b).start()
    for b in bits[1:]:
        weights_from(0, b)

    depth = depths[me]
    first = row * slots

    def by_head(dest, vals, r):
        vals = [v.astype(BF16) for v in vals]
        for h in range(HEADS):
            dest[h, :, r * hd:(r + 2) * hd] = jnp.concatenate(
                [v[:, h * hd:(h + 1) * hd] for v in vals], axis=1
            )

    def live_at(r):
        return [live_of(depth, first + r + k) for k in range(2)]

    loads[3].wait()
    loads[4].wait()
    for r in range(0, slots, 2):
        by_head(gc, [cot[r + k].astype(F32) * l for k, l in enumerate(live_at(r))], r)
        by_head(vc, [nn(feats[r + k], wg[:, groups[0]]) for k in range(2)], r)
    for h in range(HEADS):
        part[0, h * cols:(h + 1) * cols, :] = nt(gc[h], vc[h])

    def part_rows(chunk, d):
        return pl.ds(pl.multiple_of(chunk * rows + d * half, 8), half)

    def ring_copy(s, d, u):
        chunk = (pos + ring - 1 - s) % ring if d == 0 else (pos + 1 + s) % ring
        if s == 0:
            src = part.at[u, part_rows(chunk, d)]
        else:
            src = recv.at[d, s - 1, u]
        return pltpu.make_async_remote_copy(
            src_ref=src, dst_ref=recv.at[d, s, u],
            send_sem=r_send.at[d, s, u], recv_sem=r_recv.at[d, s, u],
            device_id=(me, right if d == 0 else left), device_id_type=MESH,
        )

    def hop(s, u):
        for d in range(2):
            ring_copy(s, d, u).wait_recv()
            chunk = (pos + 2 * ring - 2 - s) % ring if d == 0 else (pos + 2 + s) % ring
            recv[d, s, u] = recv[d, s, u] + part[u, part_rows(chunk, d)]
            ring_copy(s + 1, d, u).start()

    for d in range(2):
        ring_copy(0, d, 0).start()
    weights_from(1, bits[0])
    hop(0, 0)
    for b in bits[1:]:
        weights_from(1, b)
    for r in range(0, slots, 2):
        both = [nn(feats[r + k], wg[:, groups[1]]) for k in range(2)]
        by_head(qc, [v[:, :inner] * l for v, l in zip(both, live_at(r))], r)
        by_head(kc, [v[:, inner:] for v in both], r)
        if r == 0:
            hop(1, 0)
    for h in range(HEADS):
        part[1, h * cols:(h + 1) * cols, :] = nt(qc[h], kc[h])
    for d in range(2):
        ring_copy(0, d, 1).start()

    stores = [pltpu.make_async_copy(wg, wg_out, store_sem.at[0])]
    stores[0].start()
    for s in range(ring - 2):
        if s + 2 < ring - 2:
            hop(s + 2, 0)
        hop(s, 1)

    norm = lax.broadcast_in_dim(depth.astype(F32) * float(hd), (8, 128), ())
    scale = (1.0 / jnp.sqrt(norm))[0:1, 0:1]
    last = ring - 2

    def finish(d):
        for u in range(2):
            ring_copy(last, d, u).wait_recv()
        at = part_rows(pos, d)
        dprobs = recv[d, last, 0] + part[0, at]
        logits = (recv[d, last, 1] + part[1, at]) * scale
        top = jnp.max(logits, axis=-1, keepdims=True)
        expo = jnp.exp(logits - top)
        probs = expo / jnp.sum(expo, axis=-1, keepdims=True)
        mean = jnp.sum(probs * dprobs, axis=-1, keepdims=True)
        return probs.astype(BF16), (probs * (dprobs - mean) * scale).astype(BF16)

    grow = rows // gsub

    def pd_rows(chunk, g):
        return pl.ds(pl.multiple_of(chunk * rows + g * grow, 16), grow)

    def chunk_from(s, d):
        return (pos + ring - s) % ring if d == 0 else (pos + s) % ring

    def spread_copy(s, d, g):
        ref = pd.at[pd_rows(chunk_from(s, d), g)]
        return pltpu.make_async_remote_copy(
            src_ref=ref, dst_ref=ref,
            send_sem=g_send.at[d, s, g], recv_sem=g_recv.at[d, s, g],
            device_id=(me, right if d == 0 else left), device_id_type=MESH,
        )

    def sends(s, d, g):
        if s < lines - 1:
            return True
        return s == lines - 1 and d == g

    if gsub == 2:
        for d in range(2):
            probs, dlog = finish(d)
            pd[pd_rows(pos, d), 0:cols] = probs
            pd[pd_rows(pos, d), cols:2 * cols] = dlog
            for e in range(2):
                if sends(0, e, d):
                    spread_copy(0, e, d).start()
    else:
        a, b = finish(0), finish(1)
        pd[pd_rows(pos, 0), 0:cols] = jnp.concatenate([a[0], b[0]], axis=0)
        pd[pd_rows(pos, 0), cols:2 * cols] = jnp.concatenate([a[1], b[1]], axis=0)
        for e in range(2):
            if sends(0, e, 0):
                spread_copy(0, e, 0).start()

    def arrive(s):
        for g in range(gsub):
            for e in range(2):
                if sends(s, e, g):
                    spread_copy(s, e, g).wait_recv()
                    if sends(s + 1, e, g):
                        spread_copy(s + 1, e, g).start()

    def head(h):
        at = pl.ds(pl.multiple_of(h * cols, cols), cols)
        probs = pd[at, 0:cols]
        dlog = pd[at, cols:2 * cols]
        made[0, h] = nn(probs, vc[h]).astype(BF16)
        made[1, h] = nn(dlog, kc[h]).astype(BF16)
        made[2, h] = tn(dlog, qc[h]).astype(BF16)
        made[3, h] = tn(probs, gc[h]).astype(BF16)

    for s in range(lines - 1):
        arrive(s)
    far = (pos + lines) % ring
    after = (far * rows + rows - 1) // cols + 1
    for k in range(HEADS - 2):
        head((after + k) % HEADS)
    arrive(lines - 1)
    for k in range(HEADS - 2, HEADS):
        head((after + k) % HEADS)

    for r in range(slots):
        cut = slice(r * hd, (r + 1) * hd)
        live = live_of(depth, first + r)
        for h in range(0, HEADS, 2):
            both = [
                jnp.concatenate([made[i, h, :, cut], made[i, h + 1, :, cut]], axis=1)
                for i in range(4)
            ]
            att[r, :, h * hd:(h + 2) * hd] = (both[0].astype(F32) * live).astype(BF16)
            for i in range(3):
                lanes = slice(i * inner + h * hd, i * inner + (h + 2) * hd)
                stacked[r, :, lanes] = both[i + 1]
        for i, (src, dst) in enumerate(((att, att_out), (stacked, stacked_out))):
            c = pltpu.make_async_copy(src.at[r], dst.at[r], store_sem.at[1 + 2 * r + i])
            c.start()
            stores.append(c)

    for t in range(2):
        for m, b in pairs:
            weight_copy(t, m, b).wait_send()
    for s in range(ring - 1):
        for u in range(2):
            for d in range(2):
                ring_copy(s, d, u).wait_send()
    for s in range(lines):
        for g in range(gsub):
            for e in range(2):
                if sends(s, e, g):
                    spread_copy(s, e, g).wait_send()
    for c in stores:
        c.wait()


def output_kernel(att_in, stacked, wg, depths, att, grad):
    slots = pl.num_programs(0)
    depth = depths[lax.axis_index("dp")]
    slot = lax.axis_index("row") * slots + pl.program_id(0)
    att[0, 0] = att_in[0]
    grad[0, 0] = (nt(stacked[0], wg[...]) * live_of(depth, slot)).astype(BF16)


def local(dp, ring, features, cotangent, projections, depths):
    _, slots, cols, width = features.shape
    inner = projections.shape[2]
    wide = slots * (inner // HEADS)
    rows = HEADS * cols // ring
    gsub = 2 if rows % 32 == 0 else 1
    _, pairs = gather_copies(dp)
    hbm = pl.BlockSpec(memory_space=pltpu.HBM)
    anyspace = pl.BlockSpec(memory_space=pl.ANY)
    smem = pl.BlockSpec(memory_space=pltpu.SMEM)
    weights = (width, 3 * inner)
    pairshape = (HEADS * cols, 2 * cols)
    lines = ring // 2
    dma = pltpu.SemaphoreType.DMA
    att, stacked, wg = pl.pallas_call(
        functools.partial(tied_kernel, dp, ring, gsub),
        out_shape=(
            jax.ShapeDtypeStruct((slots, cols, inner), BF16),
            jax.ShapeDtypeStruct((slots, cols, 3 * inner), BF16),
            jax.ShapeDtypeStruct(weights, BF16),
        ),
        in_specs=[hbm, hbm, hbm, smem],
        out_specs=[anyspace] * 3,
        scratch_shapes=[
            pltpu.VMEM((slots, cols, width), BF16),
            pltpu.VMEM((slots, cols, inner), BF16),
            pltpu.VMEM(weights, BF16),
            *[pltpu.VMEM((HEADS, cols, wide), BF16)] * 4,
            pltpu.VMEM((2, HEADS * cols, cols), F32),
            pltpu.VMEM((2, ring - 1, 2, rows // 2, cols), F32),
            pltpu.VMEM(pairshape, BF16),
            pltpu.VMEM((4, HEADS, cols, wide), BF16),
            pltpu.VMEM((slots, cols, inner), BF16),
            pltpu.VMEM((slots, cols, 3 * inner), BF16),
            dma((5,)),
            dma((1 + 2 * slots,)),
            dma((2, len(pairs))),
            dma((2, len(pairs))),
            dma((2, ring - 1, 2)),
            dma((2, ring - 1, 2)),
            dma((2, lines, gsub)),
            dma((2, lines, gsub)),
        ],
        compiler_params=pltpu.CompilerParams(
            collective_id=0, has_side_effects=True, vmem_limit_bytes=58 * 2**20
        ),
    )(features, cotangent, projections, depths)
    return pl.pallas_call(
        output_kernel,
        grid=(slots,),
        out_shape=(
            jax.ShapeDtypeStruct((1, slots, cols, inner), BF16),
            jax.ShapeDtypeStruct((1, slots, cols, width), BF16),
        ),
        in_specs=[
            pl.BlockSpec((1, cols, inner), lambda r: (r, 0, 0)),
            pl.BlockSpec((1, cols, 3 * inner), lambda r: (r, 0, 0)),
            pl.BlockSpec(weights, lambda r: (0, 0)),
            smem,
        ],
        out_specs=[
            pl.BlockSpec((1, 1, cols, inner), lambda r: (0, r, 0, 0)),
            pl.BlockSpec((1, 1, cols, width), lambda r: (0, r, 0, 0)),
        ],
        compiler_params=pltpu.CompilerParams(vmem_limit_bytes=60 * 2**20),
    )(att, stacked, wg, depths)


def solution(mesh):
    return jax.shard_map(
        functools.partial(local, mesh.shape["dp"], mesh.shape["row"]),
        mesh=mesh,
        in_specs=(P("dp", "row", None, None), P("dp", "row", None, None), P(None, "dp", None), P()),
        out_specs=(P("dp", "row", None, None), P("dp", "row", None, None)),
        check_vma=False,
    )
```

```python
import functools

import jax
import jax.numpy as jnp
from jax import lax
from jax.experimental import pallas as pl
from jax.experimental.pallas import tpu as pltpu
from jax.sharding import PartitionSpec as P

HEADS = 6
F32 = jnp.float32
BF16 = jnp.bfloat16
MESH = pl.DeviceIdType.MESH
LAST = (((1,), (1,)), ((), ()))
FIRST = (((0,), (0,)), ((), ()))


def nt(a, b):
    return lax.dot_general(a, b, LAST, preferred_element_type=F32)


def tn(a, b):
    return lax.dot_general(a, b, FIRST, preferred_element_type=F32)


def nn(a, b):
    return jnp.dot(a, b, preferred_element_type=F32)


def gather_copies(dp):
    bits = []
    b = dp // 2
    while b:
        bits.append(b)
        b //= 2
    pairs = []
    for k, b in enumerate(bits):
        masks = [0]
        for hi in bits[:k]:
            masks += [m | hi for m in masks]
        pairs += [(m, b) for m in masks]
    return bits, pairs


def flip(me, mask):
    b = 1
    out = me
    while b <= mask:
        if mask & b:
            out = out + b - 2 * b * (lax.div(me, b) % 2)
        b *= 2
    return out


def live_of(depth, slot):
    return (slot < depth).astype(F32)


def tied_kernel(
    dp, ring, gsub,
    feats_hbm, cot_hbm, proj_hbm, depths,
    att_out, stacked_out, wg_out,
    feats, cot, wg, qc, kc, vc, gc, part, recv, pd, made, att, stacked,
    load_sem, store_sem, w_send, w_recv, r_send, r_recv, g_send, g_recv,
):
    me = lax.axis_index("dp")
    row = lax.axis_index("row")
    slots, cols, _ = feats.shape
    inner = cot.shape[2]
    hd = inner // HEADS
    shard = proj_hbm.shape[1]
    rows = part.shape[1] // ring
    half = rows // 2
    lines = ring // 2

    def row_at(pos):
        z0 = pos
        z1 = ring - 1 - pos
        low = (pos < lines).astype(jnp.int32)
        return low * (2 * z0) + (1 - low) * (2 * z1 + 1)

    z = row // 2
    x = row % 2
    pos = z + x * (ring - 1 - 2 * z)
    right = row_at((pos + 1) % ring)
    left = row_at((pos + ring - 1) % ring)

    groups = (slice(2 * inner, 3 * inner), slice(0, 2 * inner))

    def shard_at(idx, lanes):
        return wg.at[pl.ds(pl.multiple_of(idx * shard, shard), shard), lanes]

    loads = [
        pltpu.make_async_copy(
            proj_hbm.at[p], shard_at(me, slice(p * inner, (p + 1) * inner)), load_sem.at[p]
        )
        for p in range(3)
    ]
    loads.append(pltpu.make_async_copy(feats_hbm.at[0], feats, load_sem.at[3]))
    loads.append(pltpu.make_async_copy(cot_hbm.at[0], cot, load_sem.at[4]))
    for c in (loads[2], loads[0], loads[1], loads[3], loads[4]):
        c.start()

    bits, pairs = gather_copies(dp)
    barrier = pltpu.get_barrier_semaphore()
    for b in bits:
        pl.semaphore_signal(barrier, inc=1, device_id=(flip(me, b), row), device_id_type=MESH)
    for n in (left, right):
        pl.semaphore_signal(barrier, inc=1, device_id=(me, n), device_id_type=MESH)
    pl.semaphore_wait(barrier, len(bits) + 2)

    def weight_copy(t, m, b):
        i = pairs.index((m, b))
        src = shard_at(flip(me, m), groups[t])
        return pltpu.make_async_remote_copy(
            src_ref=src, dst_ref=src, send_sem=w_send.at[t, i], recv_sem=w_recv.at[t, i],
            device_id=(flip(me, b), row), device_id_type=MESH,
        )

    def weights_from(t, b):
        for m, at in pairs:
            if at == b:
                weight_copy(t, m, b).wait_recv()
                for lower in bits:
                    if lower < b:
                        weight_copy(t, m | b, lower).start()

    loads[2].wait()
    for b in bits:
        weight_copy(0, 0, b).start()
    weights_from(0, bits[0])
    loads[0].wait()
    loads[1].wait()
    for b in bits:
        weight_copy(1, 0, b).start()
    for b in bits[1:]:
        weights_from(0, b)

    depth = depths[me]
    first = row * slots

    def by_head(dest, vals, r):
        vals = [v.astype(BF16) for v in vals]
        for h in range(HEADS):
            dest[h, :, r * hd:(r + 2) * hd] = jnp.concatenate(
                [v[:, h * hd:(h + 1) * hd] for v in vals], axis=1
            )

    def live_at(r):
        return [live_of(depth, first + r + k) for k in range(2)]

    loads[3].wait()
    loads[4].wait()
    for r in range(0, slots, 2):
        by_head(gc, [cot[r + k].astype(F32) * l for k, l in enumerate(live_at(r))], r)
        val = nn(feats[r:r + 2].reshape(2 * cols, -1), wg[:, groups[0]])
        by_head(vc, [val[:cols], val[cols:]], r)
    for h in range(HEADS):
        part[0, h * cols:(h + 1) * cols, :] = nt(gc[h], vc[h])

    def part_rows(chunk, d):
        return pl.ds(pl.multiple_of(chunk * rows + d * half, 8), half)

    def ring_copy(s, d, u):
        chunk = (pos + ring - 1 - s) % ring if d == 0 else (pos + 1 + s) % ring
        if s == 0:
            src = part.at[u, part_rows(chunk, d)]
        else:
            src = recv.at[d, s - 1, u]
        return pltpu.make_async_remote_copy(
            src_ref=src, dst_ref=recv.at[d, s, u],
            send_sem=r_send.at[d, s, u], recv_sem=r_recv.at[d, s, u],
            device_id=(me, right if d == 0 else left), device_id_type=MESH,
        )

    def hop(s, u):
        for d in range(2):
            ring_copy(s, d, u).wait_recv()
            chunk = (pos + 2 * ring - 2 - s) % ring if d == 0 else (pos + 2 + s) % ring
            recv[d, s, u] = recv[d, s, u] + part[u, part_rows(chunk, d)]
            ring_copy(s + 1, d, u).start()

    for d in range(2):
        ring_copy(0, d, 0).start()
    weights_from(1, bits[0])
    hop(0, 0)
    for b in bits[1:]:
        weights_from(1, b)
    for r in range(0, slots, 2):
        both = nn(feats[r:r + 2].reshape(2 * cols, -1), wg[:, groups[1]])
        both = [both[:cols], both[cols:]]
        by_head(qc, [v[:, :inner] * l for v, l in zip(both, live_at(r))], r)
        by_head(kc, [v[:, inner:] for v in both], r)
        if r == 0:
            hop(1, 0)
    for h in range(HEADS):
        part[1, h * cols:(h + 1) * cols, :] = nt(qc[h], kc[h])
    for d in range(2):
        ring_copy(0, d, 1).start()

    stores = [pltpu.make_async_copy(wg, wg_out, store_sem.at[0])]
    stores[0].start()
    for s in range(ring - 2):
        if s + 2 < ring - 2:
            hop(s + 2, 0)
        hop(s, 1)

    norm = lax.broadcast_in_dim(depth.astype(F32) * float(hd), (8, 128), ())
    scale = (1.0 / jnp.sqrt(norm))[0:1, 0:1]
    last = ring - 2

    def finish(d):
        for u in range(2):
            ring_copy(last, d, u).wait_recv()
        at = part_rows(pos, d)
        dprobs = recv[d, last, 0] + part[0, at]
        logits = (recv[d, last, 1] + part[1, at]) * scale
        top = jnp.max(logits, axis=-1, keepdims=True)
        expo = jnp.exp(logits - top)
        probs = expo / jnp.sum(expo, axis=-1, keepdims=True)
        mean = jnp.sum(probs * dprobs, axis=-1, keepdims=True)
        return probs.astype(BF16), (probs * (dprobs - mean) * scale).astype(BF16)

    grow = rows // gsub

    def pd_rows(chunk, g):
        return pl.ds(pl.multiple_of(chunk * rows + g * grow, 16), grow)

    def chunk_from(s, d):
        return (pos + ring - s) % ring if d == 0 else (pos + s) % ring

    def spread_copy(s, d, g):
        ref = pd.at[pd_rows(chunk_from(s, d), g)]
        return pltpu.make_async_remote_copy(
            src_ref=ref, dst_ref=ref,
            send_sem=g_send.at[d, s, g], recv_sem=g_recv.at[d, s, g],
            device_id=(me, right if d == 0 else left), device_id_type=MESH,
        )

    def sends(s, d, g):
        if s < lines - 1:
            return True
        return s == lines - 1 and d == g

    if gsub == 2:
        for d in range(2):
            probs, dlog = finish(d)
            pd[pd_rows(pos, d), 0:cols] = probs
            pd[pd_rows(pos, d), cols:2 * cols] = dlog
            for e in range(2):
                if sends(0, e, d):
                    spread_copy(0, e, d).start()
    else:
        a, b = finish(0), finish(1)
        pd[pd_rows(pos, 0), 0:cols] = jnp.concatenate([a[0], b[0]], axis=0)
        pd[pd_rows(pos, 0), cols:2 * cols] = jnp.concatenate([a[1], b[1]], axis=0)
        for e in range(2):
            if sends(0, e, 0):
                spread_copy(0, e, 0).start()

    def arrive(s):
        for g in range(gsub):
            for e in range(2):
                if sends(s, e, g):
                    spread_copy(s, e, g).wait_recv()
                    if sends(s + 1, e, g):
                        spread_copy(s + 1, e, g).start()

    def head(h):
        at = pl.ds(pl.multiple_of(h * cols, cols), cols)
        probs = pd[at, 0:cols]
        dlog = pd[at, cols:2 * cols]
        made[0, h] = nn(probs, vc[h]).astype(BF16)
        made[1, h] = nn(dlog, kc[h]).astype(BF16)
        made[2, h] = tn(dlog, qc[h]).astype(BF16)
        made[3, h] = tn(probs, gc[h]).astype(BF16)

    for s in range(lines - 1):
        arrive(s)
    far = (pos + lines) % ring
    after = (far * rows + rows - 1) // cols + 1
    for k in range(HEADS - 2):
        head((after + k) % HEADS)
    arrive(lines - 1)
    for k in range(HEADS - 2, HEADS):
        head((after + k) % HEADS)

    for r in range(slots):
        cut = slice(r * hd, (r + 1) * hd)
        live = live_of(depth, first + r)
        for h in range(0, HEADS, 2):
            both = [
                jnp.concatenate([made[i, h, :, cut], made[i, h + 1, :, cut]], axis=1)
                for i in range(4)
            ]
            att[r, :, h * hd:(h + 2) * hd] = (both[0].astype(F32) * live).astype(BF16)
            for i in range(3):
                lanes = slice(i * inner + h * hd, i * inner + (h + 2) * hd)
                stacked[r, :, lanes] = both[i + 1]
        for i, (src, dst) in enumerate(((att, att_out), (stacked, stacked_out))):
            c = pltpu.make_async_copy(src.at[r], dst.at[r], store_sem.at[1 + 2 * r + i])
            c.start()
            stores.append(c)

    for t in range(2):
        for m, b in pairs:
            weight_copy(t, m, b).wait_send()
    for s in range(ring - 1):
        for u in range(2):
            for d in range(2):
                ring_copy(s, d, u).wait_send()
    for s in range(lines):
        for g in range(gsub):
            for e in range(2):
                if sends(s, e, g):
                    spread_copy(s, e, g).wait_send()
    for c in stores:
        c.wait()


def output_kernel(att_in, stacked, wg, depths, att, grad):
    slots, cols, wide = stacked.shape
    depth = depths[lax.axis_index("dp")]
    first = lax.axis_index("row") * slots
    att[0] = att_in[...]
    total = nt(stacked[...].reshape(slots * cols, wide), wg[...])
    for r in range(slots):
        part = total[r * cols:(r + 1) * cols]
        grad[0, r] = (part * live_of(depth, first + r)).astype(BF16)


def local(dp, ring, features, cotangent, projections, depths):
    _, slots, cols, width = features.shape
    inner = projections.shape[2]
    wide = slots * (inner // HEADS)
    rows = HEADS * cols // ring
    gsub = 2 if rows % 32 == 0 else 1
    _, pairs = gather_copies(dp)
    hbm = pl.BlockSpec(memory_space=pltpu.HBM)
    anyspace = pl.BlockSpec(memory_space=pl.ANY)
    smem = pl.BlockSpec(memory_space=pltpu.SMEM)
    weights = (width, 3 * inner)
    pairshape = (HEADS * cols, 2 * cols)
    lines = ring // 2
    dma = pltpu.SemaphoreType.DMA
    att, stacked, wg = pl.pallas_call(
        functools.partial(tied_kernel, dp, ring, gsub),
        out_shape=(
            jax.ShapeDtypeStruct((slots, cols, inner), BF16),
            jax.ShapeDtypeStruct((slots, cols, 3 * inner), BF16),
            jax.ShapeDtypeStruct(weights, BF16),
        ),
        in_specs=[hbm, hbm, hbm, smem],
        out_specs=[anyspace] * 3,
        scratch_shapes=[
            pltpu.VMEM((slots, cols, width), BF16),
            pltpu.VMEM((slots, cols, inner), BF16),
            pltpu.VMEM(weights, BF16),
            *[pltpu.VMEM((HEADS, cols, wide), BF16)] * 4,
            pltpu.VMEM((2, HEADS * cols, cols), F32),
            pltpu.VMEM((2, ring - 1, 2, rows // 2, cols), F32),
            pltpu.VMEM(pairshape, BF16),
            pltpu.VMEM((4, HEADS, cols, wide), BF16),
            pltpu.VMEM((slots, cols, inner), BF16),
            pltpu.VMEM((slots, cols, 3 * inner), BF16),
            dma((5,)),
            dma((1 + 2 * slots,)),
            dma((2, len(pairs))),
            dma((2, len(pairs))),
            dma((2, ring - 1, 2)),
            dma((2, ring - 1, 2)),
            dma((2, lines, gsub)),
            dma((2, lines, gsub)),
        ],
        compiler_params=pltpu.CompilerParams(
            collective_id=0, has_side_effects=True, vmem_limit_bytes=58 * 2**20
        ),
    )(features, cotangent, projections, depths)
    return pl.pallas_call(
        output_kernel,
        grid=(3,),
        out_shape=(
            jax.ShapeDtypeStruct((1, slots, cols, inner), BF16),
            jax.ShapeDtypeStruct((1, slots, cols, width), BF16),
        ),
        in_specs=[
            pl.BlockSpec((slots, cols, inner // 3), lambda n: (0, 0, n)),
            pl.BlockSpec((slots, cols, 3 * inner), lambda n: (0, 0, 0)),
            pl.BlockSpec((width // 3, 3 * inner), lambda n: (n, 0)),
            smem,
        ],
        out_specs=[
            pl.BlockSpec((1, slots, cols, inner // 3), lambda n: (0, 0, 0, n)),
            pl.BlockSpec((1, slots, cols, width // 3), lambda n: (0, 0, 0, n)),
        ],
        compiler_params=pltpu.CompilerParams(vmem_limit_bytes=60 * 2**20),
    )(att, stacked, wg, depths)


def solution(mesh):
    return jax.shard_map(
        functools.partial(local, mesh.shape["dp"], mesh.shape["row"]),
        mesh=mesh,
        in_specs=(P("dp", "row", None, None), P("dp", "row", None, None), P(None, "dp", None), P()),
        out_specs=(P("dp", "row", None, None), P("dp", "row", None, None)),
        check_vma=False,
    )
```

```python
import functools

import jax
import jax.numpy as jnp
from jax import lax
from jax.experimental import pallas as pl
from jax.experimental.pallas import tpu as pltpu
from jax.sharding import PartitionSpec as P

HEADS = 6
F32 = jnp.float32
BF16 = jnp.bfloat16
MESH = pl.DeviceIdType.MESH
LAST = (((1,), (1,)), ((), ()))
FIRST = (((0,), (0,)), ((), ()))


def nt(a, b):
    return lax.dot_general(a, b, LAST, preferred_element_type=F32)


def tn(a, b):
    return lax.dot_general(a, b, FIRST, preferred_element_type=F32)


def nn(a, b):
    return jnp.dot(a, b, preferred_element_type=F32)


def gather_copies(dp):
    bits = []
    b = dp // 2
    while b:
        bits.append(b)
        b //= 2
    pairs = []
    for k, b in enumerate(bits):
        masks = [0]
        for hi in bits[:k]:
            masks += [m | hi for m in masks]
        pairs += [(m, b) for m in masks]
    return bits, pairs


def flip(me, mask):
    b = 1
    out = me
    while b <= mask:
        if mask & b:
            out = out + b - 2 * b * (lax.div(me, b) % 2)
        b *= 2
    return out


def live_of(depth, slot):
    return (slot < depth).astype(F32)


def tied_kernel(
    dp, ring, gsub,
    feats_hbm, cot_hbm, proj_hbm, depths,
    att_out, stacked_out, wg_out,
    feats, cot, wg, qc, kc, vc, gc, part, recv, pd, made, att, stacked,
    load_sem, store_sem, w_send, w_recv, r_send, r_recv, g_send, g_recv,
):
    me = lax.axis_index("dp")
    row = lax.axis_index("row")
    slots, cols, _ = feats.shape
    inner = cot.shape[2]
    hd = inner // HEADS
    shard = proj_hbm.shape[1]
    rows = part.shape[1] // ring
    half = rows // 2
    lines = ring // 2

    def row_at(pos):
        z0 = pos
        z1 = ring - 1 - pos
        low = (pos < lines).astype(jnp.int32)
        return low * (2 * z0) + (1 - low) * (2 * z1 + 1)

    z = row // 2
    x = row % 2
    pos = z + x * (ring - 1 - 2 * z)
    right = row_at((pos + 1) % ring)
    left = row_at((pos + ring - 1) % ring)

    groups = (slice(2 * inner, 3 * inner), slice(0, 2 * inner))

    def shard_at(idx, lanes):
        return wg.at[pl.ds(pl.multiple_of(idx * shard, shard), shard), lanes]

    loads = [
        pltpu.make_async_copy(
            proj_hbm.at[p], shard_at(me, slice(p * inner, (p + 1) * inner)), load_sem.at[p]
        )
        for p in range(3)
    ]
    loads.append(pltpu.make_async_copy(feats_hbm.at[0], feats, load_sem.at[3]))
    loads.append(pltpu.make_async_copy(cot_hbm.at[0], cot, load_sem.at[4]))
    for c in (loads[2], loads[0], loads[1], loads[3], loads[4]):
        c.start()

    bits, pairs = gather_copies(dp)
    barrier = pltpu.get_barrier_semaphore()
    for b in bits:
        pl.semaphore_signal(barrier, inc=1, device_id=(flip(me, b), row), device_id_type=MESH)
    for n in (left, right):
        pl.semaphore_signal(barrier, inc=1, device_id=(me, n), device_id_type=MESH)
    pl.semaphore_wait(barrier, len(bits) + 2)

    def weight_copy(t, m, b):
        i = pairs.index((m, b))
        src = shard_at(flip(me, m), groups[t])
        return pltpu.make_async_remote_copy(
            src_ref=src, dst_ref=src, send_sem=w_send.at[t, i], recv_sem=w_recv.at[t, i],
            device_id=(flip(me, b), row), device_id_type=MESH,
        )

    def weights_from(t, b):
        for m, at in pairs:
            if at == b:
                weight_copy(t, m, b).wait_recv()
                for lower in bits:
                    if lower < b:
                        weight_copy(t, m | b, lower).start()

    loads[2].wait()
    for b in bits:
        weight_copy(0, 0, b).start()

    depth = depths[me]
    first = row * slots

    def by_head(dest, vals, r):
        vals = [v.astype(BF16) for v in vals]
        for h in range(HEADS):
            dest[h, :, r * hd:(r + 2) * hd] = jnp.concatenate(
                [v[:, h * hd:(h + 1) * hd] for v in vals], axis=1
            )

    def live_at(r):
        return [live_of(depth, first + r + k) for k in range(2)]

    loads[4].wait()
    for r in range(0, slots, 2):
        by_head(gc, [cot[r + k].astype(F32) * l for k, l in enumerate(live_at(r))], r)
    loads[3].wait()
    weights_from(0, bits[0])
    loads[0].wait()
    loads[1].wait()
    for b in bits:
        weight_copy(1, 0, b).start()
    for b in bits[1:]:
        weights_from(0, b)
    for r in range(0, slots, 2):
        val = nn(feats[r:r + 2].reshape(2 * cols, -1), wg[:, groups[0]])
        by_head(vc, [val[:cols], val[cols:]], r)
    for h in range(HEADS):
        part[0, h * cols:(h + 1) * cols, :] = nt(gc[h], vc[h])

    def part_rows(chunk, d):
        return pl.ds(pl.multiple_of(chunk * rows + d * half, 8), half)

    def ring_copy(s, d, u):
        chunk = (pos + ring - 1 - s) % ring if d == 0 else (pos + 1 + s) % ring
        if s == 0:
            src = part.at[u, part_rows(chunk, d)]
        else:
            src = recv.at[d, s - 1, u]
        return pltpu.make_async_remote_copy(
            src_ref=src, dst_ref=recv.at[d, s, u],
            send_sem=r_send.at[d, s, u], recv_sem=r_recv.at[d, s, u],
            device_id=(me, right if d == 0 else left), device_id_type=MESH,
        )

    def hop(s, u):
        for d in range(2):
            ring_copy(s, d, u).wait_recv()
            chunk = (pos + 2 * ring - 2 - s) % ring if d == 0 else (pos + 2 + s) % ring
            recv[d, s, u] = recv[d, s, u] + part[u, part_rows(chunk, d)]
            ring_copy(s + 1, d, u).start()

    for d in range(2):
        ring_copy(0, d, 0).start()
    weights_from(1, bits[0])
    hop(0, 0)
    for b in bits[1:]:
        weights_from(1, b)
    for r in range(0, slots, 2):
        both = nn(feats[r:r + 2].reshape(2 * cols, -1), wg[:, groups[1]])
        both = [both[:cols], both[cols:]]
        by_head(qc, [v[:, :inner] * l for v, l in zip(both, live_at(r))], r)
        by_head(kc, [v[:, inner:] for v in both], r)
        if r == 0:
            hop(1, 0)
    for h in range(HEADS):
        part[1, h * cols:(h + 1) * cols, :] = nt(qc[h], kc[h])
    for d in range(2):
        ring_copy(0, d, 1).start()

    stores = [pltpu.make_async_copy(wg, wg_out, store_sem.at[0])]
    stores[0].start()
    for s in range(ring - 2):
        if s + 2 < ring - 2:
            hop(s + 2, 0)
        hop(s, 1)

    norm = lax.broadcast_in_dim(depth.astype(F32) * float(hd), (8, 128), ())
    scale = (1.0 / jnp.sqrt(norm))[0:1, 0:1]
    last = ring - 2

    def finish(d):
        for u in range(2):
            ring_copy(last, d, u).wait_recv()
        at = part_rows(pos, d)
        dprobs = recv[d, last, 0] + part[0, at]
        logits = (recv[d, last, 1] + part[1, at]) * scale
        top = jnp.max(logits, axis=-1, keepdims=True)
        expo = jnp.exp(logits - top)
        probs = expo / jnp.sum(expo, axis=-1, keepdims=True)
        mean = jnp.sum(probs * dprobs, axis=-1, keepdims=True)
        return probs.astype(BF16), (probs * (dprobs - mean) * scale).astype(BF16)

    grow = rows // gsub

    def pd_rows(chunk, g):
        return pl.ds(pl.multiple_of(chunk * rows + g * grow, 16), grow)

    def chunk_from(s, d):
        return (pos + ring - s) % ring if d == 0 else (pos + s) % ring

    def spread_copy(s, d, g):
        ref = pd.at[pd_rows(chunk_from(s, d), g)]
        return pltpu.make_async_remote_copy(
            src_ref=ref, dst_ref=ref,
            send_sem=g_send.at[d, s, g], recv_sem=g_recv.at[d, s, g],
            device_id=(me, right if d == 0 else left), device_id_type=MESH,
        )

    def sends(s, d, g):
        if s < lines - 1:
            return True
        return s == lines - 1 and d == g

    if gsub == 2:
        for d in range(2):
            probs, dlog = finish(d)
            pd[pd_rows(pos, d), 0:cols] = probs
            pd[pd_rows(pos, d), cols:2 * cols] = dlog
            for e in range(2):
                if sends(0, e, d):
                    spread_copy(0, e, d).start()
    else:
        a, b = finish(0), finish(1)
        pd[pd_rows(pos, 0), 0:cols] = jnp.concatenate([a[0], b[0]], axis=0)
        pd[pd_rows(pos, 0), cols:2 * cols] = jnp.concatenate([a[1], b[1]], axis=0)
        for e in range(2):
            if sends(0, e, 0):
                spread_copy(0, e, 0).start()

    def arrive(s):
        for g in range(gsub):
            for e in range(2):
                if sends(s, e, g):
                    spread_copy(s, e, g).wait_recv()
                    if sends(s + 1, e, g):
                        spread_copy(s + 1, e, g).start()

    def head(h):
        at = pl.ds(pl.multiple_of(h * cols, cols), cols)
        probs = pd[at, 0:cols]
        dlog = pd[at, cols:2 * cols]
        made[0, h] = nn(probs, vc[h]).astype(BF16)
        made[1, h] = nn(dlog, kc[h]).astype(BF16)
        made[2, h] = tn(dlog, qc[h]).astype(BF16)
        made[3, h] = tn(probs, gc[h]).astype(BF16)

    for s in range(lines - 1):
        arrive(s)
    far = (pos + lines) % ring
    after = (far * rows + rows - 1) // cols + 1
    for k in range(HEADS - 2):
        head((after + k) % HEADS)
    arrive(lines - 1)
    for k in range(HEADS - 2, HEADS):
        head((after + k) % HEADS)

    for r in range(slots):
        cut = slice(r * hd, (r + 1) * hd)
        live = live_of(depth, first + r)
        for h in range(0, HEADS, 2):
            both = [
                jnp.concatenate([made[i, h, :, cut], made[i, h + 1, :, cut]], axis=1)
                for i in range(4)
            ]
            att[r, :, h * hd:(h + 2) * hd] = (both[0].astype(F32) * live).astype(BF16)
            for i in range(3):
                lanes = slice(i * inner + h * hd, i * inner + (h + 2) * hd)
                stacked[r, :, lanes] = both[i + 1]
        for i, (src, dst) in enumerate(((att, att_out), (stacked, stacked_out))):
            c = pltpu.make_async_copy(src.at[r], dst.at[r], store_sem.at[1 + 2 * r + i])
            c.start()
            stores.append(c)

    for t in range(2):
        for m, b in pairs:
            weight_copy(t, m, b).wait_send()
    for s in range(ring - 1):
        for u in range(2):
            for d in range(2):
                ring_copy(s, d, u).wait_send()
    for s in range(lines):
        for g in range(gsub):
            for e in range(2):
                if sends(s, e, g):
                    spread_copy(s, e, g).wait_send()
    for c in stores:
        c.wait()


def output_kernel(att_in, stacked, wg, depths, att, grad):
    slots, cols, wide = stacked.shape
    depth = depths[lax.axis_index("dp")]
    first = lax.axis_index("row") * slots
    att[0] = att_in[...]
    total = nt(stacked[...].reshape(slots * cols, wide), wg[...])
    for r in range(slots):
        part = total[r * cols:(r + 1) * cols]
        grad[0, r] = (part * live_of(depth, first + r)).astype(BF16)


def local(dp, ring, features, cotangent, projections, depths):
    _, slots, cols, width = features.shape
    inner = projections.shape[2]
    wide = slots * (inner // HEADS)
    rows = HEADS * cols // ring
    gsub = 2 if rows % 32 == 0 else 1
    _, pairs = gather_copies(dp)
    hbm = pl.BlockSpec(memory_space=pltpu.HBM)
    anyspace = pl.BlockSpec(memory_space=pl.ANY)
    smem = pl.BlockSpec(memory_space=pltpu.SMEM)
    weights = (width, 3 * inner)
    pairshape = (HEADS * cols, 2 * cols)
    lines = ring // 2
    dma = pltpu.SemaphoreType.DMA
    att, stacked, wg = pl.pallas_call(
        functools.partial(tied_kernel, dp, ring, gsub),
        out_shape=(
            jax.ShapeDtypeStruct((slots, cols, inner), BF16),
            jax.ShapeDtypeStruct((slots, cols, 3 * inner), BF16),
            jax.ShapeDtypeStruct(weights, BF16),
        ),
        in_specs=[hbm, hbm, hbm, smem],
        out_specs=[anyspace] * 3,
        scratch_shapes=[
            pltpu.VMEM((slots, cols, width), BF16),
            pltpu.VMEM((slots, cols, inner), BF16),
            pltpu.VMEM(weights, BF16),
            *[pltpu.VMEM((HEADS, cols, wide), BF16)] * 4,
            pltpu.VMEM((2, HEADS * cols, cols), F32),
            pltpu.VMEM((2, ring - 1, 2, rows // 2, cols), F32),
            pltpu.VMEM(pairshape, BF16),
            pltpu.VMEM((4, HEADS, cols, wide), BF16),
            pltpu.VMEM((slots, cols, inner), BF16),
            pltpu.VMEM((slots, cols, 3 * inner), BF16),
            dma((5,)),
            dma((1 + 2 * slots,)),
            dma((2, len(pairs))),
            dma((2, len(pairs))),
            dma((2, ring - 1, 2)),
            dma((2, ring - 1, 2)),
            dma((2, lines, gsub)),
            dma((2, lines, gsub)),
        ],
        compiler_params=pltpu.CompilerParams(
            collective_id=0, has_side_effects=True, vmem_limit_bytes=58 * 2**20
        ),
    )(features, cotangent, projections, depths)
    return pl.pallas_call(
        output_kernel,
        grid=(3,),
        out_shape=(
            jax.ShapeDtypeStruct((1, slots, cols, inner), BF16),
            jax.ShapeDtypeStruct((1, slots, cols, width), BF16),
        ),
        in_specs=[
            pl.BlockSpec((slots, cols, inner // 3), lambda n: (0, 0, n)),
            pl.BlockSpec((slots, cols, 3 * inner), lambda n: (0, 0, 0)),
            pl.BlockSpec((width // 3, 3 * inner), lambda n: (n, 0)),
            smem,
        ],
        out_specs=[
            pl.BlockSpec((1, slots, cols, inner // 3), lambda n: (0, 0, 0, n)),
            pl.BlockSpec((1, slots, cols, width // 3), lambda n: (0, 0, 0, n)),
        ],
        compiler_params=pltpu.CompilerParams(vmem_limit_bytes=60 * 2**20),
    )(att, stacked, wg, depths)


def solution(mesh):
    return jax.shard_map(
        functools.partial(local, mesh.shape["dp"], mesh.shape["row"]),
        mesh=mesh,
        in_specs=(P("dp", "row", None, None), P("dp", "row", None, None), P(None, "dp", None), P()),
        out_specs=(P("dp", "row", None, None), P("dp", "row", None, None)),
        check_vma=False,
    )
```
